32 devices in a mesh: depth: 4 (over x, core), tile: 8 (over z, y).
Axes of the slice: x: 2, y: 2, z: 4, core: 2. Of those that a mesh axis runs over, the one named last changes fastest.
Arguments:
- old_fields: float32 [2, 32, 512, 128], P(None, 'depth', 'tile'), may hold values from -6 to 6
- recv_block: int32 [4, 128], P('depth', 'tile'), may hold values from 0 to 511
- recv_count: int32 [4, 64], P('depth', 'tile'), may hold values from 0 to 2, as said below
- new_block: int32 [4, 128], P('depth', 'tile'), may hold values from 0 to 127
- moments: bfloat16 [4, 128, 4, 128, 128], P('depth', 'tile'), may hold values from -0.0606 to 0.0606, as said below
- new_volume: float32 [4, 1024, 128], P('depth', 'tile'), may hold values from 0.5 to 2
Outputs:
- new_fields: float32 [4, 1024, 2, 128], P('depth', 'tile')
The draws below stay inside these ranges and needn't reach their ends.
Inputs may be any that keep to these rules, and one draw needn't show every extreme that they name: `recv_count`: the tiles of some quarter of each depth group hold 2 live slots from every source tile. `moments`: component 0 (intersection volumes) is nonnegative.
All inputs are finite; a program needn't handle non-finite values.
Results may differ from the reference program's by a relative error of at most 0.003.
Values may be sent and summed in bfloat16 or wider, within the bound.
A program may use at most 128 MiB of HBM per device.

```python
import math
import jax
import jax.numpy as jnp
from jax import lax

XW = 128
LZ = 8
LY = 64
CAP = 2
NB = 512
NNEW = 128
SLOTS = 16
NZ = 32
NY = 512
N_DEPTH = 4
N_TILE = 8


def draw_recv_count(key, part):
    key = jax.random.fold_in(key, 11)
    base_key, order_key = jax.random.split(key)
    random_counts = jax.random.randint(base_key, (N_DEPTH, N_TILE, N_TILE), 0, CAP + 1)
    ranking = jax.random.permutation(order_key, N_TILE)
    crowded = ranking < max(1, N_TILE // 4)
    filled = jnp.where(crowded[None, :, None], CAP, random_counts)
    return filled.reshape(N_DEPTH, N_TILE * N_TILE).astype(jnp.int32)


def draw_moments(key, part):
    key = jax.random.fold_in(key, 23)
    volume_key, first_key = jax.random.split(key)
    volume_shape = (N_DEPTH, N_TILE * SLOTS, 1, XW, XW)
    first_shape = (N_DEPTH, N_TILE * SLOTS, 3, XW, XW)
    volumes = jax.random.uniform(volume_key, volume_shape, jnp.float32, 0.0, 0.06)
    firsts = 0.02 * jax.random.truncated_normal(first_key, -2.9, 2.9, first_shape, jnp.float32)
    return jnp.concatenate([volumes, firsts], axis=2).astype(jnp.bfloat16)


def place_ends(entries, stream_key, low, largest):
    spot = [jax.random.randint(jax.random.fold_in(stream_key, axis), (), 0, length) for axis, length in enumerate(entries.shape)]
    main_axis = entries.shape.index(max(entries.shape))
    next_to = spot[:main_axis] + [(spot[main_axis] + 1) % entries.shape[main_axis]] + spot[main_axis + 1:]
    return entries.at[tuple(spot)].set(low).at[tuple(next_to)].set(largest)


def levels(stream_key, dims, pieces, low, largest):
    gain = 1.0
    for dim, blocks in pieces:
        draws = jax.random.uniform(jax.random.fold_in(jax.random.fold_in(stream_key, 6), dim), (blocks,), jnp.float32, low / len(pieces), largest / len(pieces))
        gain = gain * jnp.repeat(jnp.exp(draws), dims[dim] // blocks).reshape((-1,) + (1,) * (len(dims) - 1 - dim))
    return gain


def gaussian(key, shape, scale, bound, shards=(), kind=jnp.bfloat16):
    values = scale * jax.random.normal(key, shape, jnp.float32)
    if shards:
        values = values * levels(key, shape, shards, -0.22, 0.18)
    return jnp.clip(values, -bound, bound).astype(kind)


def setup_inputs(seed: int = 0) -> dict:
    streams_of = jax.random.split(jax.random.key(seed), 7)
    old_fields = gaussian(streams_of[0], (2, NZ, NY, XW), 1.0, 6.0, ((1, 4), (2, 8)), jnp.float32)
    recv_block = place_ends(jax.random.randint(streams_of[1], (N_DEPTH, N_TILE * SLOTS), 0, NB), jax.random.fold_in(streams_of[1], 1), 0, NB - 1).astype(jnp.int32)
    recv_count = draw_recv_count(jax.random.fold_in(streams_of[6], 71), 0)
    new_block = place_ends(jax.random.randint(streams_of[3], (N_DEPTH, N_TILE * SLOTS), 0, NNEW), jax.random.fold_in(streams_of[3], 1), 0, NNEW - 1).astype(jnp.int32)
    moments = draw_moments(jax.random.fold_in(streams_of[6], 71), 0)
    new_volume = jnp.clip(jnp.exp(math.log(2.0) - 1.3862944 * jax.random.uniform(streams_of[5], (N_DEPTH, N_TILE * NNEW, XW), jnp.float32) ** levels(streams_of[5], (N_DEPTH, N_TILE * NNEW, XW), ((0, 4), (1, 8)), -0.2, 0.2)), 0.5, 2.0)
    return {"old_fields": old_fields, "recv_block": recv_block, "recv_count": recv_count, "new_block": new_block, "moments": moments, "new_volume": new_volume}


def minmod(left_value, right_value):
    return 0.5 * (jnp.sign(left_value) + jnp.sign(right_value)) * jnp.minimum(jnp.abs(left_value), jnp.abs(right_value))


def limited(centre, upper_side, lower_side):
    central = 0.5 * (upper_side - lower_side)
    return minmod(central, minmod(2.0 * (centre - lower_side), 2.0 * (upper_side - centre)))


def slope_along(values_in, along):
    length = values_in.shape[along]
    widths = [(0, 0), (0, 0), (0, 0), (0, 0)]
    widths[along] = (1, 1)
    padded = jnp.pad(values_in, widths)
    upper_side = lax.slice_in_dim(padded, 2, length + 2, axis=along)
    lower_side = lax.slice_in_dim(padded, 0, length, axis=along)
    position = jnp.arange(length, dtype=jnp.int32)
    keep_mask = ((position > 0) & (position < length - 1)).astype(jnp.float32)
    shape_keep = [1, 1, 1, 1]
    shape_keep[along] = length
    return limited(values_in, upper_side, lower_side) * keep_mask.reshape(shape_keep)


def reference(old_fields, recv_block, recv_count, new_block, moments, new_volume):
    slope_depth = slope_along(old_fields, 1)
    slope_lateral = slope_along(old_fields, 2)
    slope_x = slope_along(old_fields, 3)
    stacked = jnp.stack([old_fields, slope_depth, slope_lateral, slope_x], 0)
    stacked = stacked.transpose(2, 3, 0, 1, 4).astype(jnp.bfloat16)
    blocks = stacked.reshape(N_DEPTH, LZ, N_TILE, LY, 8, XW).transpose(0, 2, 1, 3, 4, 5)
    blocks = blocks.reshape(N_DEPTH, N_TILE, LZ * LY, 8, XW)

    def one_tile(which):
        zero = jnp.zeros((), jnp.int32)
        group_index = (which // N_TILE).astype(jnp.int32)
        tile_index = (which % N_TILE).astype(jnp.int32)
        slot_start = (tile_index * SLOTS).astype(jnp.int32)
        count_start = (tile_index * N_TILE).astype(jnp.int32)
        new_start = (tile_index * NNEW).astype(jnp.int32)
        group = lax.dynamic_index_in_dim(blocks, group_index, 0, keepdims=False)
        block_ids = lax.dynamic_slice(recv_block, (group_index, slot_start), (1, SLOTS))[0].astype(jnp.int32)
        counts = lax.dynamic_slice(recv_count, (group_index, count_start), (1, N_TILE))[0].astype(jnp.int32)
        source = jnp.arange(SLOTS, dtype=jnp.int32) // CAP
        fetched = group[source, block_ids]
        alive_mask = (jnp.arange(SLOTS, dtype=jnp.int32) % CAP < counts[source]).astype(jnp.float32)
        weights = lax.dynamic_slice(moments, (group_index, slot_start, zero, zero, zero), (1, SLOTS, 4, XW, XW))[0]
        contribution = jnp.einsum("jcno,jcfo->jfn", weights.astype(jnp.float32),
                                  fetched.reshape(SLOTS, 4, 2, XW).astype(jnp.float32),
                                  precision=lax.Precision.HIGHEST)
        contribution = contribution * alive_mask[:, None, None]
        targets = lax.dynamic_slice(new_block, (group_index, slot_start), (1, SLOTS))[0].astype(jnp.int32)
        one_hot = (targets[None, :] == jnp.arange(NNEW, dtype=jnp.int32)[:, None]).astype(jnp.float32)
        summed = jnp.dot(one_hot, contribution.reshape(SLOTS, 2 * XW), precision=lax.Precision.HIGHEST)
        volume = lax.dynamic_slice(new_volume, (group_index, new_start, zero), (1, NNEW, XW))[0]
        return summed.reshape(NNEW, 2, XW) / volume[:, None, :]

    result = lax.map(one_tile, jnp.arange(N_DEPTH * N_TILE, dtype=jnp.int32))
    return result.reshape(N_DEPTH, N_TILE * NNEW, 2, XW)
```

```python
import functools

import jax
import jax.numpy as jnp
from jax import lax
from jax.experimental import pallas as pl
from jax.experimental.pallas import tpu as pltpu
from jax.sharding import PartitionSpec as P

CAP = 2
ROWS = 8
EDGE = 8
MESH = pl.DeviceIdType.MESH


def limited(centre, upper_side, lower_side):
    central = 0.5 * (upper_side - lower_side)
    left = 2.0 * (centre - lower_side)
    right = 2.0 * (upper_side - centre)
    low = jnp.minimum(central, jnp.minimum(left, right))
    high = jnp.maximum(central, jnp.maximum(left, right))
    return jnp.maximum(low, 0.0) + jnp.minimum(high, 0.0)


def kernel(
    n_depth, n_tile,
    fields, blocks, counts, targets, moments,
    out,
    pad, asked, count_s, target_s, weights, sending, states, partial,
    local_sem, ask_send, ask_recv, halo_send, halo_recv, state_send, state_recv,
):
    layers, lateral, width = fields.shape[1:]
    slots = blocks.shape[1]
    depth = lax.axis_index("depth")
    me = lax.axis_index("tile")

    load_fields = pltpu.make_async_copy(
        fields, pad.at[:, pl.ds(1, layers), pl.ds(EDGE, lateral), :], local_sem.at[0]
    )
    load_asked = pltpu.make_async_copy(blocks, asked.at[me], local_sem.at[1])
    load_count = pltpu.make_async_copy(counts, count_s, local_sem.at[2])
    load_target = pltpu.make_async_copy(targets, target_s, local_sem.at[3])
    load_weights = pltpu.make_async_copy(moments, weights, local_sem.at[4])
    load_asked.start()
    load_fields.start()
    load_count.start()
    load_target.start()
    load_weights.start()

    barrier = pltpu.get_barrier_semaphore()

    def greet(step, carry):
        peer = lax.rem(me + step, n_tile)
        pl.semaphore_signal(barrier, inc=1, device_id=(depth, peer), device_id_type=MESH)
        return carry

    lax.fori_loop(1, n_tile, greet, 0)

    @pl.when(depth > 0)
    def _():
        pl.semaphore_signal(barrier, inc=1, device_id=(depth - 1, me), device_id_type=MESH)

    @pl.when(depth < n_depth - 1)
    def _():
        pl.semaphore_signal(barrier, inc=1, device_id=(depth + 1, me), device_id_type=MESH)

    edges = (depth > 0).astype(jnp.int32) + (depth < n_depth - 1).astype(jnp.int32)
    pl.semaphore_wait(barrier, n_tile - 1 + edges)

    def ask(peer, slot):
        return pltpu.make_async_remote_copy(
            src_ref=blocks, dst_ref=asked.at[slot],
            send_sem=ask_send.at[peer], recv_sem=ask_recv.at[slot],
            device_id=(depth, peer), device_id_type=MESH,
        )

    def halo(which, source, target, device):
        return pltpu.make_async_remote_copy(
            src_ref=source, dst_ref=target,
            send_sem=halo_send.at[which], recv_sem=halo_recv.at[which],
            device_id=device, device_id_type=MESH,
        )

    def answer(peer, slot):
        return pltpu.make_async_remote_copy(
            src_ref=sending.at[peer], dst_ref=states.at[slot],
            send_sem=state_send.at[peer], recv_sem=state_recv.at[slot],
            device_id=(depth, peer), device_id_type=MESH,
        )

    inner = pl.ds(EDGE, lateral)
    body = pl.ds(1, layers)
    halos = (
        (depth < n_depth - 1, depth > 0, halo(
            0, fields.at[:, layers - 1], pad.at[:, 0, inner, :],
            (lax.rem(depth + 1, n_depth), me))),
        (depth > 0, depth < n_depth - 1, halo(
            1, fields.at[:, 0], pad.at[:, layers + 1, inner, :],
            (lax.rem(depth + n_depth - 1, n_depth), me))),
        (me < n_tile - 1, me > 0, halo(
            2, fields.at[:, :, pl.ds(lateral - EDGE, EDGE), :], pad.at[:, body, pl.ds(0, EDGE), :],
            (depth, lax.rem(me + 1, n_tile)))),
        (me > 0, me < n_tile - 1, halo(
            3, fields.at[:, :, pl.ds(0, EDGE), :], pad.at[:, body, pl.ds(EDGE + lateral, EDGE), :],
            (depth, lax.rem(me + n_tile - 1, n_tile)))),
    )

    def ask_step(step, carry):
        ask(lax.rem(me + step, n_tile), me).start()
        return carry

    lax.fori_loop(1, n_tile, ask_step, 0)
    for sends, _, copy in halos:
        pl.when(sends)(copy.start)

    load_count.wait()
    load_target.wait()
    columns = slots * ROWS
    lane = lax.broadcasted_iota(jnp.int32, (2 * EDGE, columns), 1)
    new_of = jnp.zeros((2 * EDGE, columns), jnp.int32)
    live = jnp.zeros((2 * EDGE, columns), jnp.int32)
    for j in range(slots):
        new_of = jnp.where(lane // ROWS == j, target_s[0, j], new_of)
    for s in range(n_tile):
        live = jnp.where(lane // (ROWS * CAP) == s, count_s[0, s], live)
    row_of = jnp.where(lane // ROWS % CAP < live, 2 * new_of + lane % 2, -1)
    row_of = jnp.broadcast_to(row_of[:1], (out.shape[0], columns))
    line = lax.broadcasted_iota(jnp.int32, (out.shape[0], columns), 0)
    one_hot = jnp.where(row_of == line, 1.0, 0.0).astype(jnp.bfloat16)

    load_fields.wait()

    @pl.when(depth == 0)
    def _():
        pad[:, 0, inner, :] = pad[:, 1, inner, :]

    @pl.when(depth == n_depth - 1)
    def _():
        pad[:, layers + 1, inner, :] = pad[:, layers, inner, :]

    @pl.when(me == 0)
    def _():
        pad[:, body, pl.ds(EDGE - 1, 1), :] = pad[:, body, pl.ds(EDGE, 1), :]

    @pl.when(me == n_tile - 1)
    def _():
        pad[:, body, pl.ds(EDGE + lateral, 1), :] = pad[:, body, pl.ds(EDGE + lateral - 1, 1), :]

    for _, receives, copy in halos:
        pl.when(receives)(copy.wait_recv)
    load_asked.wait()

    x = lax.broadcasted_iota(jnp.int32, (2, width), 1)
    x_inside = (x > 0) & (x < width - 1)

    def state_of(peer):
        pieces = []
        for c in range(CAP):
            number = asked[peer, 0, CAP * me + c]
            z = lax.div(number, lateral) + 1
            y = lax.rem(number, lateral) + EDGE
            centre, below, above, before, after = (
                pad[:, z + dz, pl.ds(y + dy, 1), :].reshape(2, width)
                for dz, dy in ((0, 0), (-1, 0), (1, 0), (0, -1), (0, 1))
            )
            along_x = limited(centre, pltpu.roll(centre, width - 1, 1), pltpu.roll(centre, 1, 1))
            pieces += [
                centre,
                limited(centre, above, below),
                limited(centre, after, before),
                jnp.where(x_inside, along_x, 0.0),
            ]
        return jnp.concatenate(pieces, axis=0).astype(jnp.bfloat16)

    def answer_step(step, carry):
        peer = lax.rem(me + step, n_tile)
        ask(peer, peer).wait_recv()
        sending[peer] = state_of(peer)
        answer(peer, me).start()
        return carry

    lax.fori_loop(1, n_tile, answer_step, 0)
    states[me] = state_of(me)

    load_weights.wait()
    kind = lax.broadcasted_iota(jnp.int32, (CAP * ROWS, width), 0) // 2

    def sum_step(step, carry):
        source = lax.rem(me + step, n_tile)

        @pl.when(step > 0)
        def _():
            answer(source, source).wait_recv()

        state = states[source]
        zero = jnp.zeros_like(state)
        left = jnp.concatenate(
            [jnp.where(kind == i, state, zero) for i in range(CAP * 4)], axis=1
        )
        right = jnp.concatenate(
            [weights[0, CAP * source + i // 4, i % 4] for i in range(CAP * 4)], axis=1
        )
        first = pl.multiple_of(source * (CAP * ROWS), CAP * ROWS)
        partial[pl.ds(first, CAP * ROWS), :] = lax.dot_general(
            left, right, (((1,), (1,)), ((), ())), preferred_element_type=jnp.float32
        )
        return carry

    lax.fori_loop(0, n_tile, sum_step, 0)

    total = partial[...]
    high = total.astype(jnp.bfloat16)
    low = (total - high.astype(jnp.float32)).astype(jnp.bfloat16)
    out[...] = jnp.dot(one_hot, high, preferred_element_type=jnp.float32) + jnp.dot(
        one_hot, low, preferred_element_type=jnp.float32
    )

    for sends, _, copy in halos:
        pl.when(sends)(copy.wait_send)

    def finish(step, carry):
        peer = lax.rem(me + step, n_tile)
        ask(peer, me).wait_send()
        answer(peer, me).wait_send()
        return carry

    lax.fori_loop(1, n_tile, finish, 0)


def per_device(n_depth, n_tile, old_fields, recv_block, recv_count, new_block, moments, new_volume):
    fields, layers, lateral, width = old_fields.shape
    slots = recv_block.shape[1]
    new_count = new_volume.shape[1]
    anywhere = pl.BlockSpec(memory_space=pl.ANY)
    summed = pl.pallas_call(
        functools.partial(kernel, n_depth, n_tile),
        out_shape=jax.ShapeDtypeStruct((2 * new_count, width), jnp.float32),
        in_specs=[anywhere] * 5,
        out_specs=pl.BlockSpec(memory_space=pltpu.VMEM),
        scratch_shapes=[
            pltpu.VMEM((fields, layers + 2, lateral + 2 * EDGE, width), jnp.float32),
            pltpu.SMEM((n_tile, 1, slots), jnp.int32),
            pltpu.SMEM(recv_count.shape, jnp.int32),
            pltpu.SMEM(new_block.shape, jnp.int32),
            pltpu.VMEM(moments.shape, jnp.bfloat16),
            pltpu.VMEM((n_tile, CAP * ROWS, width), jnp.bfloat16),
            pltpu.VMEM((n_tile, CAP * ROWS, width), jnp.bfloat16),
            pltpu.VMEM((slots * ROWS, width), jnp.float32),
            pltpu.SemaphoreType.DMA((5,)),
            pltpu.SemaphoreType.DMA((n_tile,)),
            pltpu.SemaphoreType.DMA((n_tile,)),
            pltpu.SemaphoreType.DMA((4,)),
            pltpu.SemaphoreType.DMA((4,)),
            pltpu.SemaphoreType.DMA((n_tile,)),
            pltpu.SemaphoreType.DMA((n_tile,)),
        ],
        compiler_params=pltpu.CompilerParams(
            collective_id=0, has_side_effects=True, vmem_limit_bytes=63 * 2**20
        ),
    )(old_fields, recv_block, recv_count, new_block, moments)
    result = summed.reshape(new_count, 2, width) / new_volume[0][:, None, :]
    return result[None]


def solution(mesh):
    placed = (
        P(None, "depth", "tile", None),
        P("depth", "tile"),
        P("depth", "tile"),
        P("depth", "tile"),
        P("depth", "tile", None, None, None),
        P("depth", "tile", None),
    )
    return jax.shard_map(
        functools.partial(per_device, mesh.shape["depth"], mesh.shape["tile"]),
        mesh=mesh,
        in_specs=placed,
        out_specs=P("depth", "tile", None, None),
        check_vma=False,
    )
```

```python
import functools

import jax
import jax.numpy as jnp
from jax import lax
from jax.experimental import pallas as pl
from jax.experimental.pallas import tpu as pltpu
from jax.sharding import PartitionSpec as P

CAP = 2
ROWS = 8
EDGE = 8
MESH = pl.DeviceIdType.MESH


def limited(centre, upper_side, lower_side):
    central = 0.5 * (upper_side - lower_side)
    left = 2.0 * (centre - lower_side)
    right = 2.0 * (upper_side - centre)
    low = jnp.minimum(central, jnp.minimum(left, right))
    high = jnp.maximum(central, jnp.maximum(left, right))
    return jnp.maximum(low, 0.0) + jnp.minimum(high, 0.0)


def against(left, right):
    return lax.dot_general(
        left, right, (((1,), (1,)), ((), ())), preferred_element_type=jnp.float32
    )


def kernel(
    n_depth, n_tile,
    fields, blocks, counts, targets, moments, volume,
    out,
    pad, ends, beside, asked, weights, count_s, target_s, volume_v, volume_2, partial, sending, states,
    local_sem, ask_send, ask_recv, halo_send, halo_recv, state_send, state_recv,
):
    layers, lateral, width = fields.shape[1:]
    slots = blocks.shape[1]
    depth = lax.axis_index("depth")
    me = lax.axis_index("tile")
    inner = pl.ds(EDGE, lateral)
    body = pl.ds(1, layers)

    load_fields = pltpu.make_async_copy(
        fields, pad.at[:, pl.ds(1, layers), pl.ds(EDGE, lateral), :], local_sem.at[0]
    )
    load_asked = pltpu.make_async_copy(blocks, asked.at[me], local_sem.at[1])
    load_count = pltpu.make_async_copy(counts, count_s, local_sem.at[3])
    load_target = pltpu.make_async_copy(targets, target_s, local_sem.at[4])
    load_volume = pltpu.make_async_copy(volume, volume_v, local_sem.at[5])
    load_weights = pltpu.make_async_copy(moments, weights, local_sem.at[2])
    def other(step):
        return step + (step >= me).astype(jnp.int32)

    barrier = pltpu.get_barrier_semaphore()

    def greet(step, carry):
        peer = other(step)
        pl.semaphore_signal(barrier, inc=1, device_id=(depth, peer), device_id_type=MESH)
        return carry

    lax.fori_loop(0, n_tile - 1, greet, 0)

    @pl.when(depth > 0)
    def _():
        pl.semaphore_signal(barrier, inc=1, device_id=(depth - 1, me), device_id_type=MESH)

    @pl.when(depth < n_depth - 1)
    def _():
        pl.semaphore_signal(barrier, inc=1, device_id=(depth + 1, me), device_id_type=MESH)

    load_asked.start()
    load_fields.start()
    load_weights.start()
    load_count.start()
    load_target.start()
    load_volume.start()

    load_fields.wait()
    ends[0] = pad[:, body, EDGE, :]
    ends[1] = pad[:, body, EDGE + lateral - 1, :]

    edges = (depth > 0).astype(jnp.int32) + (depth < n_depth - 1).astype(jnp.int32)
    pl.semaphore_wait(barrier, n_tile - 1 + edges)

    def ask(peer, slot):
        return pltpu.make_async_remote_copy(
            src_ref=blocks, dst_ref=asked.at[slot],
            send_sem=ask_send.at[peer], recv_sem=ask_recv.at[slot],
            device_id=(depth, peer), device_id_type=MESH,
        )

    def halo(which, source, target, device):
        return pltpu.make_async_remote_copy(
            src_ref=source, dst_ref=target,
            send_sem=halo_send.at[which], recv_sem=halo_recv.at[which],
            device_id=device, device_id_type=MESH,
        )

    def answer(peer, slot):
        return pltpu.make_async_remote_copy(
            src_ref=sending.at[peer], dst_ref=states.at[slot],
            send_sem=state_send.at[peer], recv_sem=state_recv.at[slot],
            device_id=(depth, peer), device_id_type=MESH,
        )

    halos = (
        (depth < n_depth - 1, depth > 0, halo(
            0, fields.at[:, layers - 1], pad.at[:, 0, inner, :],
            (lax.rem(depth + 1, n_depth), me))),
        (depth > 0, depth < n_depth - 1, halo(
            1, fields.at[:, 0], pad.at[:, layers + 1, inner, :],
            (lax.rem(depth + n_depth - 1, n_depth), me))),
        (me < n_tile - 1, me > 0, halo(
            2, ends.at[1], beside.at[0],
            (depth, lax.rem(me + 1, n_tile)))),
        (me > 0, me < n_tile - 1, halo(
            3, ends.at[0], beside.at[1],
            (depth, lax.rem(me + n_tile - 1, n_tile)))),
    )

    def ask_step(step, carry):
        ask(other(n_tile - 2 - step), me).start()
        return carry

    lax.fori_loop(0, n_tile - 1, ask_step, 0)
    for sends, _, copy in halos:
        pl.when(sends)(copy.start)

    load_count.wait()
    load_target.wait()
    load_volume.wait()
    slots = blocks.shape[1]
    half = volume.shape[1]
    volume_2[pl.ds(0, half, stride=2), :] = volume_v[0]
    volume_2[pl.ds(1, half, stride=2), :] = volume_v[0]
    columns = slots * ROWS
    lane = lax.broadcasted_iota(jnp.int32, (2 * EDGE, columns), 1)
    new_of = jnp.zeros((2 * EDGE, columns), jnp.int32)
    live = jnp.zeros((2 * EDGE, columns), jnp.int32)
    for j in range(slots):
        new_of = jnp.where(lane // ROWS == j, target_s[0, j], new_of)
    for s in range(n_tile):
        live = jnp.where(lane // (ROWS * CAP) == s, count_s[0, s], live)
    row_of = jnp.where(lane // ROWS % CAP < live, 2 * new_of + lane % 2, -1)
    row_of = jnp.broadcast_to(row_of[:1], (out.shape[0], columns))
    line = lax.broadcasted_iota(jnp.int32, (out.shape[0], columns), 0)
    one_hot = jnp.where(row_of == line, 1.0, 0.0).astype(jnp.bfloat16)

    @pl.when(depth == 0)
    def _():
        pad[:, 0, inner, :] = pad[:, 1, inner, :]

    @pl.when(depth == n_depth - 1)
    def _():
        pad[:, layers + 1, inner, :] = pad[:, layers, inner, :]

    @pl.when(me == 0)
    def _():
        pad[:, body, EDGE - 1, :] = ends[0]

    @pl.when(me == n_tile - 1)
    def _():
        pad[:, body, EDGE + lateral, :] = ends[1]

    @pl.when(me > 0)
    def _():
        halos[2][2].wait_recv()
        pad[:, body, EDGE - 1, :] = beside[0]

    @pl.when(me < n_tile - 1)
    def _():
        halos[3][2].wait_recv()
        pad[:, body, EDGE + lateral, :] = beside[1]

    load_asked.wait()
    for _, receives, copy in halos[:2]:
        pl.when(receives)(copy.wait_recv)

    x = lax.broadcasted_iota(jnp.int32, (ROWS, width), 1)
    x_inside = (x > 0) & (x < width - 1)
    part = lax.broadcasted_iota(jnp.int32, (ROWS, width), 0)
    of_field = part % 2 == 0
    part = part // 2

    def rows(z, y):
        first, second = (
            jnp.broadcast_to(pad[f, z, pl.ds(y, 1), :], (ROWS, width)) for f in range(2)
        )
        return jnp.where(of_field, first, second)

    def state_of(peer):
        pieces = []
        for c in range(CAP):
            number = asked[peer, 0, CAP * me + c]
            z = lax.div(number, lateral) + 1
            y = lax.rem(number, lateral) + EDGE
            centre = rows(z, y)
            upper = jnp.where(part == 1, rows(z + 1, y), rows(z, y + 1))
            lower = jnp.where(part == 1, rows(z - 1, y), rows(z, y - 1))
            upper = jnp.where(part == 3, pltpu.roll(centre, width - 1, 1), upper)
            lower = jnp.where(part == 3, pltpu.roll(centre, 1, 1), lower)
            slope = limited(centre, upper, lower)
            slope = jnp.where((part < 3) | x_inside, slope, 0.0)
            pieces.append(jnp.where(part == 0, centre, slope))
        return jnp.concatenate(pieces, axis=0).astype(jnp.bfloat16)

    def answer_step(step, carry):
        peer = other(step)
        ask(peer, peer).wait_recv()
        sending[peer] = state_of(peer)
        answer(peer, me).start()
        return carry

    lax.fori_loop(0, n_tile - 1, answer_step, 0)
    states[me] = state_of(me)

    load_weights.wait()
    kind = lax.broadcasted_iota(jnp.int32, (CAP * ROWS, width), 0) // 2

    def sum_over(source):
        state = states[source]
        zero = jnp.zeros_like(state)
        left = jnp.concatenate(
            [jnp.where(kind == i, state, zero) for i in range(CAP * 4)], axis=1
        )
        right = jnp.concatenate(
            [weights[0, CAP * source + i // 4, i % 4] for i in range(CAP * 4)], axis=1
        )
        first = pl.multiple_of(source * (CAP * ROWS), CAP * ROWS)
        partial[pl.ds(first, CAP * ROWS), :] = against(left, right)

    def sum_step(step, carry):
        source = other(step)
        answer(source, source).wait_recv()
        sum_over(source)
        return carry

    sum_over(me)
    lax.fori_loop(0, n_tile - 1, sum_step, 0)

    total = partial[...]
    high = total.astype(jnp.bfloat16)
    low = (total - high.astype(jnp.float32)).astype(jnp.bfloat16)
    summed = jnp.dot(one_hot, high, preferred_element_type=jnp.float32) + jnp.dot(
        one_hot, low, preferred_element_type=jnp.float32
    )
    out[...] = summed / volume_2[...]

    for sends, _, copy in halos:
        pl.when(sends)(copy.wait_send)

    def finish(step, carry):
        peer = other(step)
        ask(peer, me).wait_send()
        answer(peer, me).wait_send()
        return carry

    lax.fori_loop(0, n_tile - 1, finish, 0)


def per_device(n_depth, n_tile, old_fields, recv_block, recv_count, new_block, moments, new_volume):
    fields, layers, lateral, width = old_fields.shape
    slots = recv_block.shape[1]
    new_count = new_volume.shape[1]
    anywhere = pl.BlockSpec(memory_space=pltpu.HBM)
    result = pl.pallas_call(
        functools.partial(kernel, n_depth, n_tile),
        out_shape=pltpu.VMEM((2 * new_count, width), jnp.float32),
        in_specs=[anywhere] * 6,
        out_specs=pl.BlockSpec(memory_space=pltpu.VMEM),
        scratch_shapes=[
            pltpu.VMEM((fields, layers + 2, lateral + 2 * EDGE, width), jnp.float32),
            pltpu.VMEM((2, fields, layers, width), jnp.float32),
            pltpu.VMEM((2, fields, layers, width), jnp.float32),
            pltpu.SMEM((n_tile, 1, slots), jnp.int32),
            pltpu.VMEM(moments.shape, jnp.bfloat16),
            pltpu.SMEM(recv_count.shape, jnp.int32),
            pltpu.SMEM(new_block.shape, jnp.int32),
            pltpu.VMEM(new_volume.shape, jnp.float32),
            pltpu.VMEM((2 * new_count, width), jnp.float32),
            pltpu.VMEM((slots * ROWS, width), jnp.float32),
            pltpu.VMEM((n_tile, CAP * ROWS, width), jnp.bfloat16),
            pltpu.VMEM((n_tile, CAP * ROWS, width), jnp.bfloat16),
            pltpu.SemaphoreType.DMA((6,)),
            pltpu.SemaphoreType.DMA((n_tile,)),
            pltpu.SemaphoreType.DMA((n_tile,)),
            pltpu.SemaphoreType.DMA((4,)),
            pltpu.SemaphoreType.DMA((4,)),
            pltpu.SemaphoreType.DMA((n_tile,)),
            pltpu.SemaphoreType.DMA((n_tile,)),
        ],
        compiler_params=pltpu.CompilerParams(
            collective_id=0, has_side_effects=True, vmem_limit_bytes=56 * 2**20
        ),
    )(old_fields, recv_block, recv_count, new_block, moments, new_volume)
    return result.reshape(1, new_count, 2, width)


def solution(mesh):
    placed = (
        P(None, "depth", "tile", None),
        P("depth", "tile"),
        P("depth", "tile"),
        P("depth", "tile"),
        P("depth", "tile", None, None, None),
        P("depth", "tile", None),
    )
    return jax.shard_map(
        functools.partial(per_device, mesh.shape["depth"], mesh.shape["tile"]),
        mesh=mesh,
        in_specs=placed,
        out_specs=P("depth", "tile", None, None),
        check_vma=False,
    )
```

```python
import functools

import jax
import jax.numpy as jnp
from jax import lax
from jax.experimental import pallas as pl
from jax.experimental.pallas import tpu as pltpu
from jax.sharding import PartitionSpec as P

CAP = 2
ROWS = 8
EDGE = 8
MESH = pl.DeviceIdType.MESH


def limited(centre, upper_side, lower_side):
    central = 0.5 * (upper_side - lower_side)
    left = 2.0 * (centre - lower_side)
    right = 2.0 * (upper_side - centre)
    low = jnp.minimum(central, jnp.minimum(left, right))
    high = jnp.maximum(central, jnp.maximum(left, right))
    return jnp.maximum(low, 0.0) + jnp.minimum(high, 0.0)


def against(left, right):
    return lax.dot_general(
        left, right, (((1,), (1,)), ((), ())), preferred_element_type=jnp.float32
    )


def kernel(
    n_depth, n_tile,
    fields, blocks, counts, targets, moments, volume,
    out,
    pad, ends, beside, asked, weights, count_s, target_s, volume_v, volume_2, partial, sending, states,
    local_sem, ask_send, ask_recv, halo_send, halo_recv, state_send, state_recv,
):
    layers, lateral, width = fields.shape[1:]
    slots = blocks.shape[1]
    depth = lax.axis_index("depth")
    me = lax.axis_index("tile")
    inner = pl.ds(EDGE, lateral)
    body = pl.ds(1, layers)

    load_fields = pltpu.make_async_copy(
        fields, pad.at[:, pl.ds(1, layers), pl.ds(EDGE, lateral), :], local_sem.at[0]
    )
    load_asked = pltpu.make_async_copy(blocks, asked.at[me], local_sem.at[1])
    load_count = pltpu.make_async_copy(counts, count_s, local_sem.at[3])
    load_target = pltpu.make_async_copy(targets, target_s, local_sem.at[4])
    load_volume = pltpu.make_async_copy(volume, volume_v, local_sem.at[5])
    load_weights = pltpu.make_async_copy(moments, weights, local_sem.at[2])
    def other(step):
        return step + (step >= me).astype(jnp.int32)

    barrier = pltpu.get_barrier_semaphore()

    def greet(step, carry):
        peer = other(step)
        pl.semaphore_signal(barrier, inc=1, device_id=(depth, peer), device_id_type=MESH)
        return carry

    lax.fori_loop(0, n_tile - 1, greet, 0)

    @pl.when(depth > 0)
    def _():
        pl.semaphore_signal(barrier, inc=1, device_id=(depth - 1, me), device_id_type=MESH)

    @pl.when(depth < n_depth - 1)
    def _():
        pl.semaphore_signal(barrier, inc=1, device_id=(depth + 1, me), device_id_type=MESH)

    load_asked.start()
    load_fields.start()
    load_count.start()
    load_target.start()
    load_volume.start()

    edges = (depth > 0).astype(jnp.int32) + (depth < n_depth - 1).astype(jnp.int32)
    pl.semaphore_wait(barrier, n_tile - 1 + edges)

    def ask(peer, slot):
        return pltpu.make_async_remote_copy(
            src_ref=blocks, dst_ref=asked.at[slot],
            send_sem=ask_send.at[peer], recv_sem=ask_recv.at[slot],
            device_id=(depth, peer), device_id_type=MESH,
        )

    def halo(which, source, target, device):
        return pltpu.make_async_remote_copy(
            src_ref=source, dst_ref=target,
            send_sem=halo_send.at[which], recv_sem=halo_recv.at[which],
            device_id=device, device_id_type=MESH,
        )

    def answer(peer, slot):
        return pltpu.make_async_remote_copy(
            src_ref=sending.at[peer], dst_ref=states.at[slot],
            send_sem=state_send.at[peer], recv_sem=state_recv.at[slot],
            device_id=(depth, peer), device_id_type=MESH,
        )

    halos = (
        (depth < n_depth - 1, depth > 0, halo(
            0, fields.at[:, layers - 1], pad.at[:, 0, inner, :],
            (lax.rem(depth + 1, n_depth), me))),
        (depth > 0, depth < n_depth - 1, halo(
            1, fields.at[:, 0], pad.at[:, layers + 1, inner, :],
            (lax.rem(depth + n_depth - 1, n_depth), me))),
        (me < n_tile - 1, me > 0, halo(
            2, ends.at[1], beside.at[0],
            (depth, lax.rem(me + 1, n_tile)))),
        (me > 0, me < n_tile - 1, halo(
            3, ends.at[0], beside.at[1],
            (depth, lax.rem(me + n_tile - 1, n_tile)))),
    )

    def ask_step(step, carry):
        ask(other(n_tile - 2 - step), me).start()
        return carry

    lax.fori_loop(0, n_tile - 1, ask_step, 0)
    load_fields.wait()
    ends[0] = pad[:, body, EDGE, :]
    ends[1] = pad[:, body, EDGE + lateral - 1, :]
    for sends, _, copy in halos:
        pl.when(sends)(copy.start)
    load_weights.start()

    load_count.wait()
    load_target.wait()
    load_volume.wait()
    slots = blocks.shape[1]
    half = volume.shape[1]
    volume_2[pl.ds(0, half, stride=2), :] = volume_v[0]
    volume_2[pl.ds(1, half, stride=2), :] = volume_v[0]
    columns = slots * ROWS
    lane = lax.broadcasted_iota(jnp.int32, (2 * EDGE, columns), 1)
    new_of = jnp.zeros((2 * EDGE, columns), jnp.int32)
    live = jnp.zeros((2 * EDGE, columns), jnp.int32)
    for j in range(slots):
        new_of = jnp.where(lane // ROWS == j, target_s[0, j], new_of)
    for s in range(n_tile):
        live = jnp.where(lane // (ROWS * CAP) == s, count_s[0, s], live)
    row_of = jnp.where(lane // ROWS % CAP < live, 2 * new_of + lane % 2, -1)
    row_of = jnp.broadcast_to(row_of[:1], (out.shape[0], columns))
    line = lax.broadcasted_iota(jnp.int32, (out.shape[0], columns), 0)
    one_hot = jnp.where(row_of == line, 1.0, 0.0).astype(jnp.bfloat16)

    @pl.when(depth == 0)
    def _():
        pad[:, 0, inner, :] = pad[:, 1, inner, :]

    @pl.when(depth == n_depth - 1)
    def _():
        pad[:, layers + 1, inner, :] = pad[:, layers, inner, :]

    @pl.when(me == 0)
    def _():
        pad[:, body, EDGE - 1, :] = ends[0]

    @pl.when(me == n_tile - 1)
    def _():
        pad[:, body, EDGE + lateral, :] = ends[1]

    @pl.when(me > 0)
    def _():
        halos[2][2].wait_recv()
        pad[:, body, EDGE - 1, :] = beside[0]

    @pl.when(me < n_tile - 1)
    def _():
        halos[3][2].wait_recv()
        pad[:, body, EDGE + lateral, :] = beside[1]

    load_asked.wait()
    for _, receives, copy in halos[:2]:
        pl.when(receives)(copy.wait_recv)

    x = lax.broadcasted_iota(jnp.int32, (ROWS, width), 1)
    x_inside = (x > 0) & (x < width - 1)
    part = lax.broadcasted_iota(jnp.int32, (ROWS, width), 0)
    of_field = part % 2 == 0
    part = part // 2

    def rows(z, y):
        first, second = (
            jnp.broadcast_to(pad[f, z, pl.ds(y, 1), :], (ROWS, width)) for f in range(2)
        )
        return jnp.where(of_field, first, second)

    def state_of(peer):
        pieces = []
        for c in range(CAP):
            number = asked[peer, 0, CAP * me + c]
            z = lax.div(number, lateral) + 1
            y = lax.rem(number, lateral) + EDGE
            centre = rows(z, y)
            upper = jnp.where(part == 1, rows(z + 1, y), rows(z, y + 1))
            lower = jnp.where(part == 1, rows(z - 1, y), rows(z, y - 1))
            upper = jnp.where(part == 3, pltpu.roll(centre, width - 1, 1), upper)
            lower = jnp.where(part == 3, pltpu.roll(centre, 1, 1), lower)
            slope = limited(centre, upper, lower)
            slope = jnp.where((part < 3) | x_inside, slope, 0.0)
            pieces.append(jnp.where(part == 0, centre, slope))
        return jnp.concatenate(pieces, axis=0).astype(jnp.bfloat16)

    def answer_step(step, carry):
        peer = other(step)
        ask(peer, peer).wait_recv()
        sending[peer] = state_of(peer)
        answer(peer, me).start()
        return carry

    lax.fori_loop(0, n_tile - 1, answer_step, 0)
    states[me] = state_of(me)

    load_weights.wait()
    kind = lax.broadcasted_iota(jnp.int32, (CAP * ROWS, width), 0) // 2

    def sum_over(source):
        state = states[source]
        zero = jnp.zeros_like(state)
        left = jnp.concatenate(
            [jnp.where(kind == i, state, zero) for i in range(CAP * 4)], axis=1
        )
        right = jnp.concatenate(
            [weights[0, CAP * source + i // 4, i % 4] for i in range(CAP * 4)], axis=1
        )
        first = pl.multiple_of(source * (CAP * ROWS), CAP * ROWS)
        partial[pl.ds(first, CAP * ROWS), :] = against(left, right)

    def sum_step(step, carry):
        source = other(step)
        answer(source, source).wait_recv()
        sum_over(source)
        return carry

    sum_over(me)
    lax.fori_loop(0, n_tile - 1, sum_step, 0)

    total = partial[...]
    high = total.astype(jnp.bfloat16)
    low = (total - high.astype(jnp.float32)).astype(jnp.bfloat16)
    summed = jnp.dot(
        jnp.concatenate([one_hot, one_hot], axis=1),
        jnp.concatenate([high, low], axis=0),
        preferred_element_type=jnp.float32,
    )
    out[...] = summed / volume_2[...]

    for sends, _, copy in halos:
        pl.when(sends)(copy.wait_send)

    def finish(step, carry):
        peer = other(step)
        ask(peer, me).wait_send()
        answer(peer, me).wait_send()
        return carry

    lax.fori_loop(0, n_tile - 1, finish, 0)


def per_device(n_depth, n_tile, old_fields, recv_block, recv_count, new_block, moments, new_volume):
    fields, layers, lateral, width = old_fields.shape
    slots = recv_block.shape[1]
    new_count = new_volume.shape[1]
    anywhere = pl.BlockSpec(memory_space=pltpu.HBM)
    result = pl.pallas_call(
        functools.partial(kernel, n_depth, n_tile),
        out_shape=pltpu.VMEM((2 * new_count, width), jnp.float32),
        in_specs=[anywhere] * 6,
        out_specs=pl.BlockSpec(memory_space=pltpu.VMEM),
        scratch_shapes=[
            pltpu.VMEM((fields, layers + 2, lateral + 2 * EDGE, width), jnp.float32),
            pltpu.VMEM((2, fields, layers, width), jnp.float32),
            pltpu.VMEM((2, fields, layers, width), jnp.float32),
            pltpu.SMEM((n_tile, 1, slots), jnp.int32),
            pltpu.VMEM(moments.shape, jnp.bfloat16),
            pltpu.SMEM(recv_count.shape, jnp.int32),
            pltpu.SMEM(new_block.shape, jnp.int32),
            pltpu.VMEM(new_volume.shape, jnp.float32),
            pltpu.VMEM((2 * new_count, width), jnp.float32),
            pltpu.VMEM((slots * ROWS, width), jnp.float32),
            pltpu.VMEM((n_tile, CAP * ROWS, width), jnp.bfloat16),
            pltpu.VMEM((n_tile, CAP * ROWS, width), jnp.bfloat16),
            pltpu.SemaphoreType.DMA((6,)),
            pltpu.SemaphoreType.DMA((n_tile,)),
            pltpu.SemaphoreType.DMA((n_tile,)),
            pltpu.SemaphoreType.DMA((4,)),
            pltpu.SemaphoreType.DMA((4,)),
            pltpu.SemaphoreType.DMA((n_tile,)),
            pltpu.SemaphoreType.DMA((n_tile,)),
        ],
        compiler_params=pltpu.CompilerParams(
            collective_id=0, has_side_effects=True, vmem_limit_bytes=56 * 2**20
        ),
    )(old_fields, recv_block, recv_count, new_block, moments, new_volume)
    return result.reshape(1, new_count, 2, width)


def solution(mesh):
    placed = (
        P(None, "depth", "tile", None),
        P("depth", "tile"),
        P("depth", "tile"),
        P("depth", "tile"),
        P("depth", "tile", None, None, None),
        P("depth", "tile", None),
    )
    return jax.shard_map(
        functools.partial(per_device, mesh.shape["depth"], mesh.shape["tile"]),
        mesh=mesh,
        in_specs=placed,
        out_specs=P("depth", "tile", None, None),
        check_vma=False,
    )
```
